1024 devices in a mesh: fsdp: 128 (over z_lo, y, x), tensor: 8 (over z_hi, core).
Axes of the slice: x: 4, y: 8, z: 16 (z_hi: 4, z_lo: 4; z = z_hi * 4 + z_lo), core: 2. Of those that a mesh axis runs over, the one named last changes fastest.
Arguments:
- hidden_act: bfloat16 [128, 27648], P('fsdp', 'tensor'), may hold values from -0.59765625 to 0.59765625
- out_grad: bfloat16 [128, 16384], P('fsdp'), may hold values from -6 to 6
- down_weight: bfloat16 [27648, 16384], P('tensor', 'fsdp'), may hold values from -0.046875 to 0.046875
Outputs:
- weight_grad: bfloat16 [27648, 16384], P('tensor', 'fsdp')
- hidden_grad: bfloat16 [128, 27648], P('fsdp', 'tensor')
The draws below stay inside these ranges and needn't reach their ends.
All inputs are finite; a program needn't handle non-finite values.
Results may differ from the reference program's by a relative error of at most 0.0049.
Values may be sent and summed in bfloat16 or wider, within the bound.
No kernel may reach another device: no remote copies, remote signals or barrier semaphores. Data moves between devices by JAX's collectives and lax.ppermute only.
A program may use at most 32 MiB of HBM per device.

```python
import jax
import jax.numpy as jnp
import numpy as np
from jax import lax

D = 16384
FF = 27648
BLOCK = 128
TOKENS = 128
N_TENSOR = 8


def steps_of(key, extent, cuts, smallest, high):
    def one(axis_at, blocks):
        draws = jax.random.uniform(jax.random.fold_in(jax.random.fold_in(key, 6), axis_at), (blocks,), jnp.float32, smallest / len(cuts), high / len(cuts))
        return jnp.repeat(jnp.exp(draws), extent[axis_at] // blocks).reshape((-1,) + (1,) * (len(extent) - axis_at - 1))

    level = one(*cuts[0])
    for cut in cuts[1:]:
        level = level * one(*cut)
    return level


def noise(stream_key, dims, scale, most, shards=(), kind=jnp.bfloat16):
    entries = jax.random.normal(stream_key, dims, jnp.float32) * scale
    if len(shards) > 0:
        entries = steps_of(stream_key, dims, shards, -0.22, 0.18) * entries
    return jnp.clip(entries, min=-most, max=most).astype(kind)


def setup_inputs(seed: int = 0) -> dict:
    key_of = jax.random.split(jax.random.key(seed), 4)
    return {
        "hidden_act": noise(key_of[0], (TOKENS, FF), 0.1, 0.59765625, ((0, 128), (1, 8))),
        "out_grad": noise(key_of[1], (TOKENS, D), 1.0, 6.0, ((0, 128),)),
        "down_weight": noise(key_of[2], (FF, D), D ** -0.5, 0.046875, ((0, 8), (1, 128))),
    }


def walsh_table(order):
    positions = jnp.arange(order, dtype=jnp.int32)
    common = jnp.bitwise_and(positions[:, None], positions[None, :])
    parity = jnp.zeros((order, order), jnp.int32)
    for shift_count in range(order.bit_length() - 1):
        parity = parity + jnp.bitwise_and(jnp.right_shift(common, shift_count), 1)
    return (1 - 2 * (parity % 2)).astype(jnp.float32)

def rotate_rows(values):
    row_count = values.shape[0]
    shaped = values.reshape(row_count, N_TENSOR, FF // (N_TENSOR * BLOCK), BLOCK)
    cross = walsh_table(N_TENSOR)
    inner = walsh_table(BLOCK)
    mixed = jnp.einsum('ab,rbkc->rakc', cross, shaped, precision=lax.Precision.HIGHEST)
    mixed = jnp.einsum('rakc,cd->rakd', mixed, inner, precision=lax.Precision.HIGHEST)
    scale = 1.0 / np.sqrt(float(N_TENSOR * BLOCK))
    return (mixed * scale).reshape(row_count, FF)

def reference(hidden_act, out_grad, down_weight):
    rotated = rotate_rows(hidden_act.astype(jnp.float32)).astype(jnp.bfloat16)
    width = FF // N_TENSOR

    def one_block(index):
        piece = lax.dynamic_slice_in_dim(rotated, index * width, width, 1)
        product = lax.dot_general(piece, out_grad, (((0,), (0,)), ((), ())), preferred_element_type=jnp.float32)
        return product.astype(jnp.bfloat16)
    blocks = lax.map(one_block, jnp.arange(N_TENSOR, dtype=jnp.int32))
    weight_grad = blocks.reshape(FF, D)
    rotated_grad = lax.dot_general(out_grad, down_weight, (((1,), (1,)), ((), ())), preferred_element_type=jnp.float32)
    hidden_grad = rotate_rows(rotated_grad).astype(jnp.bfloat16)
    return (weight_grad, hidden_grad)
```

```python
import jax
import jax.numpy as jnp
import numpy as np
from jax import lax
from jax.sharding import PartitionSpec as P

BLOCK = 128


def walsh(order):
    table = np.ones((1, 1), np.float32)
    while table.shape[0] < order:
        table = np.block([[table, table], [table, -table]])
    return table


def block_factor(values, scale):
    row_count = values.shape[0]
    shaped = values.reshape(row_count, values.shape[1] // BLOCK, BLOCK)
    inner = jnp.asarray(walsh(BLOCK))
    mixed = jnp.einsum("rkc,cd->rkd", shaped, inner, precision=lax.Precision.HIGHEST)
    return (mixed * scale).reshape(row_count, values.shape[1])


def rotate_own(values, tensor_index, tensor_count):
    row_count = values.shape[0]
    shaped = values.reshape(row_count, tensor_count, values.shape[1] // tensor_count)
    signs = lax.dynamic_index_in_dim(
        jnp.asarray(walsh(tensor_count)), tensor_index, 0, keepdims=False
    )
    crossed = jnp.sum(shaped * signs[None, :, None], axis=1)
    return block_factor(crossed, 1.0 / np.sqrt(float(tensor_count * BLOCK)))


def per_device(hidden_act, out_grad, down_weight):
    tensor_count = lax.axis_size("tensor")
    tensor_index = lax.axis_index("tensor")
    fsdp_count = lax.axis_size("fsdp")
    width = hidden_act.shape[1]
    grad_cols = lax.all_to_all(out_grad, "fsdp", split_axis=1, concat_axis=0, tiled=True)
    own_full = lax.all_gather(hidden_act, "tensor", axis=1, tiled=True)
    own_rotated = rotate_own(own_full.astype(jnp.float32), tensor_index, tensor_count).astype(
        jnp.bfloat16
    )
    partial = lax.dot_general(
        grad_cols, down_weight, (((1,), (1,)), ((), ())), preferred_element_type=jnp.float32
    ).astype(jnp.bfloat16)
    sent = jnp.concatenate(
        [
            jnp.broadcast_to(own_rotated.reshape(1, width // BLOCK, BLOCK),
                             (fsdp_count, width // BLOCK, BLOCK)),
            partial.reshape(fsdp_count, width // BLOCK, BLOCK),
        ],
        axis=1,
    )
    got = lax.all_to_all(sent, "fsdp", split_axis=0, concat_axis=0, tiled=True)
    rotated = got[:, : width // BLOCK].reshape(fsdp_count, width)
    weight_grad = lax.dot_general(
        rotated, grad_cols, (((0,), (0,)), ((), ())), preferred_element_type=jnp.float32
    ).astype(jnp.bfloat16)
    grad_rows = jnp.sum(got[:, width // BLOCK :].astype(jnp.float32), axis=0).reshape(1, width)
    grad_full = lax.all_gather(grad_rows, "tensor", axis=1, tiled=True)
    hidden_grad = rotate_own(grad_full, tensor_index, tensor_count).astype(jnp.bfloat16)
    return (weight_grad, hidden_grad)


def solution(mesh):
    return jax.shard_map(
        per_device,
        mesh=mesh,
        in_specs=(P("fsdp", "tensor"), P("fsdp", None), P("tensor", "fsdp")),
        out_specs=(P("tensor", "fsdp"), P("fsdp", "tensor")),
        check_vma=False,
    )
```

```python
import jax
import jax.numpy as jnp
import numpy as np
from jax import lax
from jax.sharding import Mesh, PartitionSpec as P

BLOCK = 128
ZL, Y, X, ZH, C = 4, 8, 4, 4, 2
F32, BF16 = jnp.float32, jnp.bfloat16


def walsh(order):
    table = np.ones((1, 1), np.float32)
    while table.shape[0] < order:
        table = np.block([[table, table], [table, -table]])
    return table


def token_order():
    table = np.zeros((ZL * Y * X, ZL * Y * X), np.float32)
    for zl in range(ZL):
        for y in range(Y):
            for x in range(X):
                table[(x * Y + y) * ZL + zl, (zl * Y + y) * X + x] = 1.0
    return table


def block_factor(values):
    shaped = values.reshape(values.shape[-1] // BLOCK, BLOCK)
    mixed = jnp.dot(shaped, jnp.asarray(walsh(BLOCK)), precision=lax.Precision.HIGHEST)
    mixed = mixed * (1.0 / np.sqrt(float(ZH * C * BLOCK)))
    return mixed.astype(BF16).reshape(1, values.shape[-1])


def dot(a, b, dims):
    return lax.dot_general(a, b, (dims, ((), ())), preferred_element_type=F32)


def exchange(values, axes):
    return lax.all_to_all(values, axes, split_axis=0, concat_axis=0, tiled=True)


def butterfly(values, axis, bit):
    count = lax.axis_size(axis)
    other = lax.ppermute(values, axis, [(i, i ^ bit) for i in range(count)])
    sign = jnp.where((lax.axis_index(axis) & bit) == 0, 1.0, -1.0).astype(F32)
    return values.astype(F32) * sign + other.astype(F32)


def per_device(hidden_act, out_grad, down_weight):
    width = hidden_act.shape[1]

    grad_cols = exchange(out_grad.reshape(ZL * Y * X, 1, -1), ("zl", "y", "x"))
    grad_cols = dot(
        jnp.asarray(token_order(), BF16), grad_cols.reshape(ZL * Y * X, -1), ((1,), (0,))
    ).astype(BF16)

    crossed = butterfly(hidden_act, "zh", 1)
    crossed = butterfly(crossed, "zh", 2)
    crossed = butterfly(crossed, "c", 1)
    rotated = block_factor(crossed)

    partial = dot(grad_cols, down_weight, ((1,), (1,))).astype(BF16)
    partial = exchange(partial.reshape(X, Y * ZL, width), "x")
    partial = jnp.sum(partial.astype(F32), axis=0).astype(BF16)

    sent = jnp.concatenate(
        [jnp.broadcast_to(rotated[None], (Y * ZL, 1, width)), partial.reshape(Y * ZL, 1, width)],
        axis=1,
    )
    got = exchange(sent, ("y", "zl"))

    grad_row = jnp.sum(got[:, 1].astype(F32), axis=0)
    column = exchange(jnp.broadcast_to(grad_row, (ZH, 1, width)), "zh").reshape(ZH, width)
    signs = lax.dynamic_index_in_dim(
        jnp.asarray(walsh(ZH)), lax.axis_index("zh"), 0, keepdims=False
    )
    grad_row = jnp.sum(column * signs[:, None], axis=0)
    hidden_grad = block_factor(butterfly(grad_row, "c", 1))

    rotated = lax.all_gather(got[:, 0], "x", axis=0, tiled=True)
    weight_grad = dot(rotated, grad_cols, ((0,), (0,))).astype(BF16)
    return (weight_grad, hidden_grad)


def solution(mesh):
    fine = Mesh(mesh.devices.reshape(ZL, Y, X, ZH, C), ("zl", "y", "x", "zh", "c"))
    fsdp, tensor = ("zl", "y", "x"), ("zh", "c")
    return jax.shard_map(
        per_device,
        mesh=fine,
        in_specs=(P(fsdp, tensor), P(fsdp, None), P(tensor, fsdp)),
        out_specs=(P(tensor, fsdp), P(fsdp, tensor)),
        check_vma=False,
    )
```

```python
import jax
import jax.numpy as jnp
import numpy as np
from jax import lax
from jax.sharding import Mesh, PartitionSpec as P

BLOCK = 128
ZL, Y, X, ZH, C = 4, 8, 4, 4, 2
F32, BF16 = jnp.float32, jnp.bfloat16


def walsh(order):
    table = np.ones((1, 1), np.float32)
    while table.shape[0] < order:
        table = np.block([[table, table], [table, -table]])
    return table


def token_order():
    table = np.zeros((ZL * Y * X, ZL * Y * X), np.float32)
    for zl in range(ZL):
        for y in range(Y):
            for x in range(X):
                table[(x * Y + y) * ZL + zl, (zl * Y + y) * X + x] = 1.0
    return table


def block_factor(values):
    shaped = values.reshape(values.shape[-1] // BLOCK, BLOCK)
    mixed = jnp.dot(shaped, jnp.asarray(walsh(BLOCK)), precision=lax.Precision.HIGHEST)
    mixed = mixed * (1.0 / np.sqrt(float(ZH * C * BLOCK)))
    return mixed.astype(BF16).reshape(1, values.shape[-1])


def dot(a, b, dims):
    return lax.dot_general(a, b, (dims, ((), ())), preferred_element_type=F32)


def exchange(values, axes):
    return lax.all_to_all(values, axes, split_axis=0, concat_axis=0, tiled=True)


def butterfly(values, axis, bit):
    count = lax.axis_size(axis)
    other = lax.ppermute(values, axis, [(i, i ^ bit) for i in range(count)])
    sign = jnp.where((lax.axis_index(axis) & bit) == 0, 1.0, -1.0).astype(F32)
    return values.astype(F32) * sign + other.astype(F32)


def zh_sign(zh, step):
    common = zh & (zh ^ step)
    return jnp.where(((common ^ (common >> 1)) & 1) == 0, 1.0, -1.0).astype(F32)


def per_device(hidden_act, out_grad, down_weight):
    width = hidden_act.shape[1]

    grad_cols = exchange(out_grad.reshape(ZL * Y * X, 1, -1), ("zl", "y", "x"))
    grad_cols = dot(
        jnp.asarray(token_order(), BF16), grad_cols.reshape(ZL * Y * X, -1), ((1,), (0,))
    ).astype(BF16)

    crossed = butterfly(hidden_act, "c", 1)
    crossed = butterfly(crossed, "zh", 1)
    crossed = butterfly(crossed, "zh", 2)
    rotated = block_factor(crossed)

    partial = dot(grad_cols, down_weight, ((1,), (1,))).astype(BF16)
    partial = exchange(partial.reshape(X, Y * ZL, width), "x")
    partial = jnp.sum(partial.astype(F32), axis=0).astype(BF16)

    sent = jnp.concatenate(
        [jnp.broadcast_to(rotated[None], (Y * ZL, 1, width)), partial.reshape(Y * ZL, 1, width)],
        axis=1,
    )
    got = exchange(sent, ("y", "zl"))

    grad_row = jnp.sum(got[:, 1].astype(F32), axis=0, keepdims=True)
    zh = lax.axis_index("zh")
    crossed = grad_row * zh_sign(zh, 0)
    for step in range(1, ZH):
        other = lax.ppermute(grad_row, "zh", [(i, i ^ step) for i in range(ZH)])
        crossed = crossed + other * zh_sign(zh, step)
    hidden_grad = block_factor(butterfly(crossed, "c", 1))

    rotated = exchange(jnp.broadcast_to(got[:, 0], (X, Y * ZL, width)), "x")
    weight_grad = dot(rotated.reshape(X * Y * ZL, width), grad_cols, ((0,), (0,))).astype(BF16)
    return (weight_grad, hidden_grad)


def solution(mesh):
    fine = Mesh(mesh.devices.reshape(ZL, Y, X, ZH, C), ("zl", "y", "x", "zh", "c"))
    fsdp, tensor = ("zl", "y", "x"), ("zh", "c")
    return jax.shard_map(
        per_device,
        mesh=fine,
        in_specs=(P(fsdp, tensor), P(fsdp, None), P(tensor, fsdp)),
        out_specs=(P(tensor, fsdp), P(fsdp, tensor)),
        check_vma=False,
    )
```

```python
import jax
import jax.numpy as jnp
import numpy as np
from jax import lax
from jax.sharding import Mesh, PartitionSpec as P

BLOCK = 128
ZL, Y, X, ZH, C = 4, 8, 4, 4, 2
F32, BF16 = jnp.float32, jnp.bfloat16


def walsh(order):
    table = np.ones((1, 1), np.float32)
    while table.shape[0] < order:
        table = np.block([[table, table], [table, -table]])
    return table


def token_order():
    table = np.zeros((ZL * Y * X, ZL * Y * X), np.float32)
    for zl in range(ZL):
        for y in range(Y):
            for x in range(X):
                table[(x * Y + y) * ZL + zl, (zl * Y + y) * X + x] = 1.0
    return table


def block_factor(values):
    mixed = jnp.dot(values, jnp.asarray(walsh(BLOCK)), precision=lax.Precision.HIGHEST)
    return (mixed * (1.0 / np.sqrt(float(ZH * C * BLOCK)))).astype(BF16)


def dot(a, b, dims):
    return lax.dot_general(a, b, (dims, ((), ())), preferred_element_type=F32)


def exchange(values, axes):
    return lax.all_to_all(values, axes, split_axis=0, concat_axis=0, tiled=True)


def butterfly(values, axis, bit):
    count = lax.axis_size(axis)
    other = lax.ppermute(values, axis, [(i, i ^ bit) for i in range(count)])
    sign = jnp.where((lax.axis_index(axis) & bit) == 0, 1.0, -1.0).astype(F32)
    return values.astype(F32) * sign + other.astype(F32)


def zh_sign(zh, other):
    common = zh & other
    return jnp.where(((common ^ (common >> 1)) & 1) == 0, 1.0, -1.0).astype(F32)


def per_device(hidden_act, out_grad, down_weight):
    width = hidden_act.shape[1]

    grad_cols = exchange(out_grad.reshape(ZL * Y * X, 1, -1), ("zl", "y", "x"))
    grad_cols = dot(
        jnp.asarray(token_order(), BF16), grad_cols.reshape(ZL * Y * X, -1), ((1,), (0,))
    ).astype(BF16)

    crossed = butterfly(hidden_act, "zh", 1).reshape(width // BLOCK, BLOCK)
    crossed = butterfly(crossed, "zh", 2)
    crossed = butterfly(crossed, "c", 1)
    rotated = block_factor(crossed).reshape(1, 1, width)

    partial = dot(grad_cols, down_weight, ((1,), (1,))).astype(BF16)
    partial = exchange(partial.reshape(X, Y * ZL, width), "x")
    partial = jnp.sum(partial.astype(F32), axis=0).astype(BF16)

    first = lax.broadcasted_iota(jnp.int32, (Y * ZL, 2, width), 1) == 0
    sent = jnp.where(first, rotated, partial[:, None])
    got = exchange(sent, ("y", "zl"))

    grad_row = jnp.sum(got[:, 1].astype(F32), axis=0).reshape(width // BLOCK, BLOCK)
    column = exchange(jnp.broadcast_to(grad_row, (ZH, width // BLOCK, BLOCK)), "zh")
    zh = lax.axis_index("zh")
    grad_row = sum(column[i] * zh_sign(zh, i) for i in range(ZH))
    hidden_grad = block_factor(butterfly(grad_row, "c", 1)).reshape(1, width)

    rotated = lax.all_gather(got[:, 0], "x", axis=0, tiled=True)
    weight_grad = dot(rotated, grad_cols, ((0,), (0,))).astype(BF16)
    return (weight_grad, hidden_grad)


def solution(mesh):
    fine = Mesh(mesh.devices.reshape(ZL, Y, X, ZH, C), ("zl", "y", "x", "zh", "c"))
    fsdp, tensor = ("zl", "y", "x"), ("zh", "c")
    return jax.shard_map(
        per_device,
        mesh=fine,
        in_specs=(P(fsdp, tensor), P(fsdp, None), P(tensor, fsdp)),
        out_specs=(P(tensor, fsdp), P(fsdp, tensor)),
        check_vma=False,
    )
```

```python
import jax
import jax.numpy as jnp
import numpy as np
from jax import lax
from jax.sharding import Mesh, PartitionSpec as P

BLOCK = 128
ZL, Y, X, ZH, C = 4, 8, 4, 4, 2
F32, BF16 = jnp.float32, jnp.bfloat16


def walsh(order):
    table = np.ones((1, 1), np.float32)
    while table.shape[0] < order:
        table = np.block([[table, table], [table, -table]])
    return table


def token_order():
    table = np.zeros((ZL * Y * X, ZL * Y * X), np.float32)
    for zl in range(ZL):
        for y in range(Y):
            for x in range(X):
                table[(x * Y + y) * ZL + zl, (zl * Y + y) * X + x] = 1.0
    return table


def block_factor(values):
    mixed = jnp.dot(values, jnp.asarray(walsh(BLOCK)), precision=lax.Precision.HIGHEST)
    return (mixed * (1.0 / np.sqrt(float(ZH * C * BLOCK)))).astype(BF16)


def dot(a, b, dims):
    return lax.dot_general(a, b, (dims, ((), ())), preferred_element_type=F32)


def exchange(values, axes):
    return lax.all_to_all(values, axes, split_axis=0, concat_axis=0, tiled=True)


def butterfly(values, axis, bit):
    count = lax.axis_size(axis)
    other = lax.ppermute(values, axis, [(i, i ^ bit) for i in range(count)])
    sign = jnp.where((lax.axis_index(axis) & bit) == 0, 1.0, -1.0).astype(F32)
    return values.astype(F32) * sign + other.astype(F32)


def walsh_sign(own, other):
    common = own & other
    parity = (common ^ (common >> 1) ^ (common >> 2)) & 1
    return jnp.where(parity == 0, 1.0, -1.0).astype(F32)


def per_device(hidden_act, out_grad, down_weight):
    width = hidden_act.shape[1]

    grad_cols = exchange(out_grad.reshape(ZL * Y * X, 1, -1), ("zl", "y", "x"))
    grad_cols = dot(
        jnp.asarray(token_order(), BF16), grad_cols.reshape(ZL * Y * X, -1), ((1,), (0,))
    ).astype(BF16)

    crossed = butterfly(hidden_act, "zh", 1).reshape(width // BLOCK, BLOCK)
    crossed = butterfly(crossed, "zh", 2)

    partial = dot(grad_cols, down_weight, ((1,), (1,))).astype(BF16)
    partial, crossed = lax.optimization_barrier((partial, crossed))
    rotated = block_factor(butterfly(crossed, "c", 1)).reshape(1, 1, width)
    partial = exchange(partial.reshape(X, Y * ZL, width), "x")
    partial = jnp.sum(partial.astype(F32), axis=0).astype(BF16)

    first = lax.broadcasted_iota(jnp.int32, (Y * ZL, 2, width), 1) == 0
    sent = jnp.where(first, rotated, partial[:, None])
    got = exchange(sent, ("y", "zl"))

    grad_row = jnp.sum(got[:, 1].astype(F32), axis=0).reshape(width // BLOCK, BLOCK)
    column = exchange(jnp.broadcast_to(grad_row, (ZH * C, width // BLOCK, BLOCK)), ("zh", "c"))
    own = lax.axis_index(("zh", "c"))
    crossed = sum(column[i] * walsh_sign(own, i) for i in range(ZH * C))
    hidden_grad = block_factor(crossed).reshape(1, width)

    rotated = lax.all_gather(got[:, 0], "x", axis=0, tiled=True)
    weight_grad = dot(rotated, grad_cols, ((0,), (0,))).astype(BF16)
    return (weight_grad, hidden_grad)


def solution(mesh):
    fine = Mesh(mesh.devices.reshape(ZL, Y, X, ZH, C), ("zl", "y", "x", "zh", "c"))
    fsdp, tensor = ("zl", "y", "x"), ("zh", "c")
    return jax.shard_map(
        per_device,
        mesh=fine,
        in_specs=(P(fsdp, tensor), P(fsdp, None), P(tensor, fsdp)),
        out_specs=(P(tensor, fsdp), P(fsdp, tensor)),
        check_vma=False,
    )
```

```python
import jax
import jax.numpy as jnp
import numpy as np
from jax import lax
from jax.sharding import Mesh, PartitionSpec as P

BLOCK = 128
ZL, Y, X, ZH, C = 4, 8, 4, 4, 2
F32, BF16 = jnp.float32, jnp.bfloat16


def walsh(order):
    table = np.ones((1, 1), np.float32)
    while table.shape[0] < order:
        table = np.block([[table, table], [table, -table]])
    return table


def token_order():
    table = np.zeros((ZL * Y * X, ZL * Y * X), np.float32)
    for zl in range(ZL):
        for y in range(Y):
            for x in range(X):
                table[(x * Y + y) * ZL + zl, (zl * Y + y) * X + x] = 1.0
    return table


def block_factor(values):
    shaped = values.reshape(values.size // BLOCK, BLOCK)
    mixed = jnp.dot(shaped, jnp.asarray(walsh(BLOCK)), precision=lax.Precision.HIGHEST)
    mixed = mixed * (1.0 / np.sqrt(float(ZH * C * BLOCK)))
    return mixed.astype(BF16).reshape(1, values.size)


def dot(a, b, dims):
    return lax.dot_general(a, b, (dims, ((), ())), preferred_element_type=F32)


def exchange(values, axes):
    return lax.all_to_all(values, axes, split_axis=0, concat_axis=0, tiled=True)


def butterfly(values, axis, bit):
    count = lax.axis_size(axis)
    other = lax.ppermute(values, axis, [(i, i ^ bit) for i in range(count)])
    sign = jnp.where((lax.axis_index(axis) & bit) == 0, 1.0, -1.0).astype(F32)
    return values.astype(F32) * sign + other.astype(F32)


def zh_sign(zh, other):
    common = zh & other
    return jnp.where(((common ^ (common >> 1)) & 1) == 0, 1.0, -1.0).astype(F32)


def per_device(hidden_act, out_grad, down_weight):
    width = hidden_act.shape[1]

    grad_cols = exchange(out_grad.reshape(ZL * Y * X, 1, -1), ("zl", "y", "x"))
    grad_cols = dot(
        jnp.asarray(token_order(), BF16), grad_cols.reshape(ZL * Y * X, -1), ((1,), (0,))
    ).astype(BF16)

    crossed = butterfly(hidden_act, "zh", 1)
    crossed = butterfly(crossed, "zh", 2)
    crossed = butterfly(crossed, "c", 1)
    rotated = block_factor(crossed)

    partial = dot(grad_cols, down_weight, ((1,), (1,))).astype(BF16)
    partial = exchange(partial.reshape(X, Y * ZL, width), "x")
    partial = jnp.sum(partial.astype(F32), axis=0).astype(BF16)

    sent = jnp.concatenate(
        [jnp.broadcast_to(rotated[None], (Y * ZL, 1, width)), partial.reshape(Y * ZL, 1, width)],
        axis=1,
    )
    got = exchange(sent, ("y", "zl"))

    grad_row = jnp.sum(got[:, 1].astype(F32), axis=0).reshape(width // BLOCK, BLOCK)
    column = exchange(jnp.broadcast_to(grad_row, (ZH, width // BLOCK, BLOCK)), "zh")
    zh = lax.axis_index("zh")
    crossed = sum(column[i] * zh_sign(zh, i) for i in range(ZH))
    hidden_grad = block_factor(butterfly(crossed, "c", 1))

    rotated = lax.all_gather(got[:, 0], "x", axis=0, tiled=True)
    weight_grad = dot(rotated, grad_cols, ((0,), (0,))).astype(BF16)
    return (weight_grad, hidden_grad)


def solution(mesh):
    fine = Mesh(mesh.devices.reshape(ZL, Y, X, ZH, C), ("zl", "y", "x", "zh", "c"))
    fsdp, tensor = ("zl", "y", "x"), ("zh", "c")
    return jax.shard_map(
        per_device,
        mesh=fine,
        in_specs=(P(fsdp, tensor), P(fsdp, None), P(tensor, fsdp)),
        out_specs=(P(tensor, fsdp), P(fsdp, tensor)),
        check_vma=False,
    )
```

```python
import jax
import jax.numpy as jnp
import numpy as np
from jax import lax
from jax.sharding import Mesh, PartitionSpec as P

BLOCK = 128
ZL, Y, X, ZH, C = 4, 8, 4, 4, 2
F32, BF16 = jnp.float32, jnp.bfloat16


def walsh(order):
    table = np.ones((1, 1), np.float32)
    while table.shape[0] < order:
        table = np.block([[table, table], [table, -table]])
    return table


def token_order():
    table = np.zeros((ZL * Y * X, ZL * Y * X), np.float32)
    for zl in range(ZL):
        for y in range(Y):
            for x in range(X):
                table[(x * Y + y) * ZL + zl, (zl * Y + y) * X + x] = 1.0
    return table


def block_factor(values):
    shaped = values.reshape(values.size // BLOCK, BLOCK)
    mixed = jnp.dot(shaped, jnp.asarray(walsh(BLOCK)), precision=lax.Precision.HIGHEST)
    mixed = mixed * (1.0 / np.sqrt(float(ZH * C * BLOCK)))
    return mixed.astype(BF16).reshape(1, values.size)


def dot(a, b, dims):
    return lax.dot_general(a, b, (dims, ((), ())), preferred_element_type=F32)


def exchange(values, axes):
    return lax.all_to_all(values, axes, split_axis=0, concat_axis=0, tiled=True)


def butterfly(values, axis, bit):
    count = lax.axis_size(axis)
    other = lax.ppermute(values, axis, [(i, i ^ bit) for i in range(count)])
    sign = jnp.where((lax.axis_index(axis) & bit) == 0, 1.0, -1.0).astype(F32)
    return values.astype(F32) * sign + other.astype(F32)


def zh_sign(zh, other):
    common = zh & other
    return jnp.where(((common ^ (common >> 1)) & 1) == 0, 1.0, -1.0).astype(F32)


def per_device(hidden_act, out_grad, down_weight):
    width = hidden_act.shape[1]

    grad_cols = exchange(out_grad.reshape(ZL * Y * X, 1, -1), ("zl", "y", "x"))
    grad_cols = dot(
        jnp.asarray(token_order(), BF16), grad_cols.reshape(ZL * Y * X, -1), ((1,), (0,))
    ).astype(BF16)

    crossed = butterfly(hidden_act, "c", 1)
    crossed = butterfly(crossed, "zh", 2)
    crossed = butterfly(crossed, "zh", 1)
    rotated = block_factor(crossed)

    partial = dot(grad_cols, down_weight, ((1,), (1,))).astype(BF16)
    partial = exchange(partial.reshape(X, Y * ZL, width), "x")
    partial = jnp.sum(partial.astype(F32), axis=0).astype(BF16)

    sent = jnp.concatenate(
        [jnp.broadcast_to(rotated[None], (Y * ZL, 1, width)), partial.reshape(Y * ZL, 1, width)],
        axis=1,
    )
    got = exchange(sent, ("y", "zl"))

    grad_row = jnp.sum(got[:, 1].astype(F32), axis=0).reshape(width // BLOCK, BLOCK)
    column = exchange(jnp.broadcast_to(grad_row, (ZH, width // BLOCK, BLOCK)), "zh")
    zh = lax.axis_index("zh")
    crossed = sum(column[i] * zh_sign(zh, i) for i in range(ZH))
    hidden_grad = block_factor(butterfly(crossed, "c", 1))

    rotated = lax.all_gather(got[:, 0], "x", axis=0, tiled=True)
    weight_grad = dot(rotated, grad_cols, ((0,), (0,))).astype(BF16)
    return (weight_grad, hidden_grad)


def solution(mesh):
    fine = Mesh(mesh.devices.reshape(ZL, Y, X, ZH, C), ("zl", "y", "x", "zh", "c"))
    fsdp, tensor = ("zl", "y", "x"), ("zh", "c")
    return jax.shard_map(
        per_device,
        mesh=fine,
        in_specs=(P(fsdp, tensor), P(fsdp, None), P(tensor, fsdp)),
        out_specs=(P(tensor, fsdp), P(fsdp, tensor)),
        check_vma=False,
    )
```

```python
import jax
import jax.numpy as jnp
import numpy as np
from jax import lax
from jax.sharding import Mesh, PartitionSpec as P

BLOCK = 128
ZL, Y, X, ZH, C = 4, 8, 4, 4, 2
F32, BF16 = jnp.float32, jnp.bfloat16


def walsh(order):
    table = np.ones((1, 1), np.float32)
    while table.shape[0] < order:
        table = np.block([[table, table], [table, -table]])
    return table


def token_order():
    table = np.zeros((ZL * Y * X, ZL * Y * X), np.float32)
    for zl in range(ZL):
        for y in range(Y):
            for x in range(X):
                table[(x * ZL + zl) * Y + y, (zl * Y + y) * X + x] = 1.0
    return table


def block_factor(values):
    shaped = values.reshape(values.size // BLOCK, BLOCK)
    mixed = jnp.dot(shaped, jnp.asarray(walsh(BLOCK)), precision=lax.Precision.HIGHEST)
    mixed = mixed * (1.0 / np.sqrt(float(ZH * C * BLOCK)))
    return mixed.astype(BF16).reshape(1, values.size)


def dot(a, b, dims):
    return lax.dot_general(a, b, (dims, ((), ())), preferred_element_type=F32)


def exchange(values, axes):
    return lax.all_to_all(values, axes, split_axis=0, concat_axis=0, tiled=True)


def butterfly(values, axis, bit):
    count = lax.axis_size(axis)
    other = lax.ppermute(values, axis, [(i, i ^ bit) for i in range(count)])
    sign = jnp.where((lax.axis_index(axis) & bit) == 0, 1.0, -1.0).astype(F32)
    return values.astype(F32) * sign + other.astype(F32)


def zh_sign(zh, other):
    common = zh & other
    return jnp.where(((common ^ (common >> 1)) & 1) == 0, 1.0, -1.0).astype(F32)


def per_device(hidden_act, out_grad, down_weight):
    width = hidden_act.shape[1]

    grad_cols = exchange(out_grad.reshape(ZL * Y * X, 1, -1), ("zl", "y", "x"))
    grad_cols = dot(
        jnp.asarray(token_order(), BF16), grad_cols.reshape(ZL * Y * X, -1), ((1,), (0,))
    ).astype(BF16)

    crossed = butterfly(hidden_act, "c", 1)
    crossed = butterfly(crossed, "zh", 2)
    crossed = butterfly(crossed, "zh", 1)
    rotated = block_factor(crossed)

    partial = dot(grad_cols, down_weight, ((1,), (1,))).astype(BF16)
    partial = exchange(partial.reshape(X, ZL * Y, width), "x")
    partial = jnp.sum(partial.astype(F32), axis=0).astype(BF16)

    sent = jnp.concatenate(
        [jnp.broadcast_to(rotated[None], (ZL * Y, 1, width)), partial.reshape(ZL * Y, 1, width)],
        axis=1,
    )
    got = exchange(sent, ("zl", "y"))

    grad_row = jnp.sum(got[:, 1].astype(F32), axis=0).reshape(width // BLOCK, BLOCK)
    column = exchange(jnp.broadcast_to(grad_row, (ZH, width // BLOCK, BLOCK)), "zh")
    zh = lax.axis_index("zh")
    crossed = sum(column[i] * zh_sign(zh, i) for i in range(ZH))
    hidden_grad = block_factor(butterfly(crossed, "c", 1))

    rotated = lax.all_gather(got[:, 0], "x", axis=0, tiled=True)
    weight_grad = dot(rotated, grad_cols, ((0,), (0,))).astype(BF16)
    return (weight_grad, hidden_grad)


def solution(mesh):
    fine = Mesh(mesh.devices.reshape(ZL, Y, X, ZH, C), ("zl", "y", "x", "zh", "c"))
    fsdp, tensor = ("zl", "y", "x"), ("zh", "c")
    return jax.shard_map(
        per_device,
        mesh=fine,
        in_specs=(P(fsdp, tensor), P(fsdp, None), P(tensor, fsdp)),
        out_specs=(P(tensor, fsdp), P(fsdp, tensor)),
        check_vma=False,
    )
```

```python
import jax
import jax.numpy as jnp
import numpy as np
from jax import lax
from jax.sharding import Mesh, PartitionSpec as P

BLOCK = 128
ZL, Y, X, ZH, C = 4, 8, 4, 4, 2
F32, BF16 = jnp.float32, jnp.bfloat16


def walsh(order):
    table = np.ones((1, 1), np.float32)
    while table.shape[0] < order:
        table = np.block([[table, table], [table, -table]])
    return table


def block_factor(values):
    shaped = values.reshape(values.size // BLOCK, BLOCK)
    mixed = jnp.dot(shaped, jnp.asarray(walsh(BLOCK)), precision=lax.Precision.HIGHEST)
    mixed = mixed * (1.0 / np.sqrt(float(ZH * C * BLOCK)))
    return mixed.astype(BF16).reshape(1, values.size)


def dot(a, b, dims):
    return lax.dot_general(a, b, (dims, ((), ())), preferred_element_type=F32)


def exchange(values, axes):
    return lax.all_to_all(values, axes, split_axis=0, concat_axis=0, tiled=True)


def butterfly(values, axis, bit):
    count = lax.axis_size(axis)
    other = lax.ppermute(values, axis, [(i, i ^ bit) for i in range(count)])
    sign = jnp.where((lax.axis_index(axis) & bit) == 0, 1.0, -1.0).astype(F32)
    return values.astype(F32) * sign + other.astype(F32)


def zh_sign(zh, other):
    common = zh & other
    return jnp.where(((common ^ (common >> 1)) & 1) == 0, 1.0, -1.0).astype(F32)


def per_device(hidden_act, out_grad, down_weight):
    width = hidden_act.shape[1]

    pieces = out_grad.reshape(ZL, Y, X, 1, -1).transpose(2, 1, 0, 3, 4)
    grad_cols = exchange(pieces.reshape(ZL * Y * X, 1, -1), ("x", "y", "zl"))
    grad_cols = grad_cols.reshape(ZL * Y * X, -1)

    crossed = butterfly(hidden_act, "c", 1)
    crossed = butterfly(crossed, "zh", 2)
    crossed = butterfly(crossed, "zh", 1)
    rotated = block_factor(crossed)

    partial = dot(grad_cols, down_weight, ((1,), (1,))).astype(BF16)
    partial = exchange(partial.reshape(X, Y * ZL, width), "x")
    partial = jnp.sum(partial.astype(F32), axis=0).astype(BF16)

    sent = jnp.concatenate(
        [jnp.broadcast_to(rotated[None], (Y * ZL, 1, width)), partial.reshape(Y * ZL, 1, width)],
        axis=1,
    )
    got = exchange(sent, ("y", "zl"))

    grad_row = jnp.sum(got[:, 1].astype(F32), axis=0).reshape(width // BLOCK, BLOCK)
    column = exchange(jnp.broadcast_to(grad_row, (ZH, width // BLOCK, BLOCK)), "zh")
    zh = lax.axis_index("zh")
    crossed = sum(column[i] * zh_sign(zh, i) for i in range(ZH))
    hidden_grad = block_factor(butterfly(crossed, "c", 1))

    rotated = lax.all_gather(got[:, 0], "x", axis=0, tiled=True)
    weight_grad = dot(rotated, grad_cols, ((0,), (0,))).astype(BF16)
    return (weight_grad, hidden_grad)


def solution(mesh):
    fine = Mesh(mesh.devices.reshape(ZL, Y, X, ZH, C), ("zl", "y", "x", "zh", "c"))
    fsdp, tensor = ("zl", "y", "x"), ("zh", "c")
    return jax.shard_map(
        per_device,
        mesh=fine,
        in_specs=(P(fsdp, tensor), P(fsdp, None), P(tensor, fsdp)),
        out_specs=(P(tensor, fsdp), P(fsdp, tensor)),
        check_vma=False,
    )
```
